32 devices in a mesh: dp: 4 (over y, x), seq: 2 (over core), fsdp: 4 (over z).
Axes of the slice: x: 2, y: 2, z: 4, core: 2. Of those that a mesh axis runs over, the one named last changes fastest.
Arguments:
- signal: bfloat16 [16, 256, 1024], P(('dp', 'fsdp'), 'seq'), may hold values from -100 to 100
- w_query: bfloat16 [1024, 512], P('fsdp'), may hold values from -1 to 1
- w_key: bfloat16 [1024, 512], P('fsdp'), may hold values from -1 to 1
- w_value: bfloat16 [1024, 512], P('fsdp'), may hold values from -0.1875 to 0.1875
- w_output: bfloat16 [1024, 512], P('fsdp'), may hold values from -0.25 to 0.25
- upstream: bfloat16 [16, 256, 1024], P(('dp', 'fsdp'), 'seq'), may hold values from -6 to 6
Outputs:
- output: bfloat16 [16, 256, 1024], P(('dp', 'fsdp'), 'seq')
- grad_signal: bfloat16 [16, 256, 1024], P(('dp', 'fsdp'), 'seq')
- grad_query: float32 [1024, 512], P('fsdp')
- grad_key: float32 [1024, 512], P('fsdp')
- grad_value: float32 [1024, 512], P('fsdp')
- grad_output: float32 [1024, 512], P('fsdp')
The draws below stay inside these ranges and needn't reach their ends.
All inputs are finite; a program needn't handle non-finite values.
Results may differ from the reference program's by a relative error of at most 0.02.
The reference program's roundings to bfloat16 on the way (of `normed`, `queries`, `attn_weights`, `context`, `grad_context`, `grad_scores` and `grad_keys`) count: a program that leaves them out, or rounds other values in their place, can miss the bound.
Values may be sent and summed in bfloat16 or wider, within the bound.
A program may use at most 128 MiB of HBM per device.

```python
import math
import jax
import jax.numpy as jnp
from jax import lax

D = 1024
HEADS = 8
HSIZE = 64
FR_DEV = 128
HD = 512
FRAMES = 256
RECORDS = 16
TOKENS = 4096


def draw_signal(key, part):
    shape = (RECORDS, FRAMES, D)
    col_scale = jnp.exp(jax.random.uniform(jax.random.fold_in(key, 32), (D,), jnp.float32, math.log(0.3), math.log(3.0)))
    row_scale = jnp.exp(jax.random.uniform(jax.random.fold_in(key, 33), (RECORDS, FRAMES, 1), jnp.float32, math.log(0.5), math.log(1.5)))
    blocks = FRAMES // FR_DEV
    block_width = D // blocks
    order = jax.random.permutation(jax.random.fold_in(key, 34), blocks)
    frame_block = jnp.arange(FRAMES) // FR_DEV
    col_block = jnp.arange(D) // block_width
    target = (order[frame_block][None, :] + jnp.arange(RECORDS)[:, None]) % blocks
    boost = jnp.where(col_block[None, None, :] == target[:, :, None], 2.0, 1.0)
    noise = jax.random.truncated_normal(jax.random.fold_in(key, 31), -4.0, 4.0, shape, jnp.float32)
    base = noise * col_scale * boost
    return (base * row_scale).astype(jnp.bfloat16)


def draw_w_query(key, part):
    base = jax.random.truncated_normal(jax.random.fold_in(key, 21), -4.0, 4.0, (D, HD), jnp.float32) * (1.7 / math.sqrt(D))
    return base.astype(jnp.bfloat16)


def draw_w_key(key, part):
    base = jax.random.truncated_normal(jax.random.fold_in(key, 22), -4.0, 4.0, (D, HD), jnp.float32) * (1.7 / math.sqrt(D))
    return base.astype(jnp.bfloat16)


def level_of(stream_key, shape, split, low, top_value):
    gain = 1.0
    for axis_at, blocks in split:
        heights = jax.random.uniform(jax.random.fold_in(jax.random.fold_in(stream_key, 6), axis_at), (blocks,), jnp.float32, low / len(split), top_value / len(split))
        gain = gain * jnp.repeat(jnp.exp(heights), shape[axis_at] // blocks).reshape((-1,) + (1,) * (len(shape) - 1 - axis_at))
    return gain


def centred(key, shape, deviation, most, shards=(), dtype=jnp.bfloat16):
    drawn = deviation * jax.random.normal(key, shape, jnp.float32)
    if shards:
        drawn = drawn * level_of(key, shape, shards, -0.22, 0.18)
    return jnp.clip(drawn, -most, most).astype(dtype)


def setup_inputs(seed: int = 0) -> dict:
    streams_of = jax.random.split(jax.random.key(seed), 7)
    signal = draw_signal(jax.random.fold_in(streams_of[6], 71), 0)
    w_query = draw_w_query(jax.random.fold_in(streams_of[6], 71), 0)
    w_key = draw_w_key(jax.random.fold_in(streams_of[6], 71), 0)
    w_value = centred(streams_of[3], (D, HD), D ** -0.5, 0.1875, ((0, 4),))
    w_output = centred(streams_of[4], (D, HD), HD ** -0.5, 0.25, ((0, 4),))
    upstream = centred(streams_of[5], (RECORDS, FRAMES, D), 1.0, 6.0, ((0, 16), (1, 2)))
    return {"signal": signal, "w_query": w_query, "w_key": w_key, "w_value": w_value, "w_output": w_output, "upstream": upstream}


def normalize(frame_rows):
    widened = frame_rows.astype(jnp.float32)
    centre = widened - lax.optimization_barrier(jnp.mean(widened, axis=-1, keepdims=True))
    variance = lax.optimization_barrier(jnp.mean(centre * centre, axis=-1, keepdims=True))
    inverse = lax.rsqrt(variance + 1e-05)
    return (centre * inverse, inverse)

def split_heads(matrix):
    return matrix.reshape(matrix.shape[0], HEADS, HSIZE).astype(jnp.float32)

def reference(signal, w_query, w_key, w_value, w_output, upstream):
    score_scale = HSIZE ** (-0.5)

    def record(record_pair):
        frame_rows, grad_frames = record_pair
        normed_f, inverse = normalize(frame_rows)
        normed = normed_f.astype(jnp.bfloat16)
        queries = jnp.dot(normed, w_query, preferred_element_type=jnp.float32).astype(jnp.bfloat16)
        key_rows = jnp.dot(normed, w_key, preferred_element_type=jnp.float32).astype(jnp.bfloat16)
        value_rows = jnp.dot(normed, w_value, preferred_element_type=jnp.float32).astype(jnp.bfloat16)
        query_heads = split_heads(queries)
        key_heads = split_heads(key_rows)
        value_heads = split_heads(value_rows)
        scores = jnp.einsum('qhs,khs->hqk', query_heads, key_heads) * score_scale
        row_max = lax.optimization_barrier(jnp.max(scores, axis=-1, keepdims=True))
        exponent = jnp.exp(scores - row_max)
        attention = exponent / lax.optimization_barrier(jnp.sum(exponent, axis=-1, keepdims=True))
        attn_weights = attention.astype(jnp.bfloat16)
        context = jnp.einsum('hqk,khs->qhs', attn_weights.astype(jnp.float32), value_heads)
        context = context.reshape(FRAMES, HD).astype(jnp.bfloat16)
        projected = jnp.dot(context, w_output.T, preferred_element_type=jnp.float32)
        output_rows = (frame_rows.astype(jnp.float32) + projected).astype(jnp.bfloat16)
        grad_context = jnp.dot(grad_frames, w_output, preferred_element_type=jnp.float32).astype(jnp.bfloat16)
        grad_heads = split_heads(grad_context)
        grad_attention = jnp.einsum('qhs,khs->hqk', grad_heads, value_heads)
        row_delta = lax.optimization_barrier(jnp.sum(attention * grad_attention, axis=-1, keepdims=True))
        grad_scores = (attention * (grad_attention - row_delta) * score_scale).astype(jnp.bfloat16)
        wide_scores = grad_scores.astype(jnp.float32)
        grad_queries = jnp.einsum('hqk,khs->qhs', wide_scores, key_heads).reshape(FRAMES, HD).astype(jnp.bfloat16)
        grad_keys = jnp.einsum('hqk,qhs->khs', wide_scores, query_heads).reshape(FRAMES, HD).astype(jnp.bfloat16)
        grad_values = jnp.einsum('hqk,qhs->khs', attn_weights.astype(jnp.float32), grad_heads)
        grad_values = grad_values.reshape(FRAMES, HD).astype(jnp.bfloat16)
        grad_normed = jnp.dot(grad_queries, w_query.T, preferred_element_type=jnp.float32)
        grad_normed = grad_normed + jnp.dot(grad_keys, w_key.T, preferred_element_type=jnp.float32)
        grad_normed = grad_normed + jnp.dot(grad_values, w_value.T, preferred_element_type=jnp.float32)
        grad_mean = lax.optimization_barrier(jnp.mean(grad_normed, axis=-1, keepdims=True))
        grad_along = lax.optimization_barrier(jnp.mean(grad_normed * normed_f, axis=-1, keepdims=True))
        grad_rows = grad_frames.astype(jnp.float32) + inverse * (grad_normed - grad_mean - normed_f * grad_along)
        grad_rows = grad_rows.astype(jnp.bfloat16)
        terms = jnp.concatenate([jnp.dot(normed.T, grad_queries, preferred_element_type=jnp.float32), jnp.dot(normed.T, grad_keys, preferred_element_type=jnp.float32), jnp.dot(normed.T, grad_values, preferred_element_type=jnp.float32), jnp.dot(grad_frames.T, context, preferred_element_type=jnp.float32)], axis=1)
        return (output_rows, grad_rows, terms)
    output_rows, grad_rows, terms = lax.map(record, (signal, upstream))
    totals = lax.optimization_barrier(jnp.sum(terms, axis=0)) * TOKENS ** (-0.5)
    return (output_rows, grad_rows, totals[:, :HD], totals[:, HD:2 * HD], totals[:, 2 * HD:3 * HD], totals[:, 3 * HD:])
```

```python
import jax
import jax.numpy as jnp
from jax import lax
from jax.experimental import pallas as pl
from jax.experimental.pallas import tpu as pltpu
from jax.sharding import PartitionSpec as P

HEADS = 8
HSIZE = 64


def normalize(frame_rows):
    widened = frame_rows.astype(jnp.float32)
    centre = widened - jnp.mean(widened, axis=-1, keepdims=True)
    variance = jnp.mean(centre * centre, axis=-1, keepdims=True)
    inverse = lax.rsqrt(variance + 1e-05)
    return (centre * inverse, inverse)


def split_heads(matrix):
    return matrix.reshape(matrix.shape[0], HEADS, HSIZE)


def dot_across(left, right):
    return lax.dot_general(
        left, right, (((0,), (0,)), ((), ())), preferred_element_type=jnp.float32
    )


def dot_against(left, right):
    return lax.dot_general(
        left, right, (((1,), (1,)), ((), ())), preferred_element_type=jnp.float32
    )


def body(signal, w_query, w_key, w_value, w_output, upstream):
    q_weight, k_weight, v_weight, o_weight = (
        lax.all_gather(w_query, "fsdp", axis=0, tiled=True),
        lax.all_gather(w_key, "fsdp", axis=0, tiled=True),
        lax.all_gather(w_value, "fsdp", axis=0, tiled=True),
        lax.all_gather(w_output, "fsdp", axis=0, tiled=True),
    )
    score_scale = HSIZE ** (-0.5)
    frame_rows = signal[0]
    grad_frames = upstream[0]
    local_frames = frame_rows.shape[0]
    width_heads = q_weight.shape[1]
    normed_f, inverse = normalize(frame_rows)
    normed = normed_f.astype(jnp.bfloat16)
    queries = jnp.dot(normed, q_weight, preferred_element_type=jnp.float32).astype(jnp.bfloat16)
    key_rows = jnp.dot(normed, k_weight, preferred_element_type=jnp.float32).astype(jnp.bfloat16)
    value_rows = jnp.dot(normed, v_weight, preferred_element_type=jnp.float32).astype(jnp.bfloat16)
    all_keys, all_values = (
        lax.all_gather(key_rows, "seq", axis=0, tiled=True),
        lax.all_gather(value_rows, "seq", axis=0, tiled=True),
    )
    query_heads = split_heads(queries)
    key_heads = split_heads(all_keys)
    value_heads = split_heads(all_values)
    scores = (
        jnp.einsum("qhs,khs->hqk", query_heads, key_heads, preferred_element_type=jnp.float32)
        * score_scale
    )
    row_max = jnp.max(scores, axis=-1, keepdims=True)
    exponent = jnp.exp(scores - row_max)
    row_total = jnp.sum(exponent, axis=-1, keepdims=True)
    attention = exponent / row_total
    attn_weights = attention.astype(jnp.bfloat16)
    context = jnp.einsum(
        "hqk,khs->qhs", attn_weights, value_heads, preferred_element_type=jnp.float32
    )
    context = context.reshape(local_frames, width_heads).astype(jnp.bfloat16)
    projected = dot_against(context, o_weight)
    output_rows = (frame_rows.astype(jnp.float32) + projected).astype(jnp.bfloat16)
    grad_context = jnp.dot(grad_frames, o_weight, preferred_element_type=jnp.float32).astype(
        jnp.bfloat16
    )
    grad_heads = split_heads(grad_context)
    grad_attention = jnp.einsum(
        "qhs,khs->hqk", grad_heads, value_heads, preferred_element_type=jnp.float32
    )
    row_delta = jnp.sum(attention * grad_attention, axis=-1, keepdims=True)
    grad_scores = (attention * (grad_attention - row_delta) * score_scale).astype(jnp.bfloat16)
    grad_queries = jnp.einsum(
        "hqk,khs->qhs", grad_scores, key_heads, preferred_element_type=jnp.float32
    )
    grad_queries = grad_queries.reshape(local_frames, width_heads).astype(jnp.bfloat16)
    all_queries, all_grad_context = (
        lax.all_gather(queries, "seq", axis=0, tiled=True),
        lax.all_gather(grad_context, "seq", axis=0, tiled=True),
    )
    all_max, all_total, all_delta = (
        lax.all_gather(row_max, "seq", axis=1, tiled=True),
        lax.all_gather(row_total, "seq", axis=1, tiled=True),
        lax.all_gather(row_delta, "seq", axis=1, tiled=True),
    )
    far_query_heads = split_heads(all_queries)
    far_grad_heads = split_heads(all_grad_context)
    own_keys = split_heads(key_rows)
    own_values = split_heads(value_rows)
    far_scores = (
        jnp.einsum("qhs,khs->hqk", far_query_heads, own_keys, preferred_element_type=jnp.float32)
        * score_scale
    )
    far_attention = jnp.exp(far_scores - all_max) / all_total
    far_weights = far_attention.astype(jnp.bfloat16)
    far_grad = jnp.einsum(
        "qhs,khs->hqk", far_grad_heads, own_values, preferred_element_type=jnp.float32
    )
    far_scaled = (far_attention * (far_grad - all_delta) * score_scale).astype(jnp.bfloat16)
    grad_keys = jnp.einsum(
        "hqk,qhs->khs", far_scaled, far_query_heads, preferred_element_type=jnp.float32
    )
    grad_keys = grad_keys.reshape(local_frames, width_heads).astype(jnp.bfloat16)
    grad_values = jnp.einsum(
        "hqk,qhs->khs", far_weights, far_grad_heads, preferred_element_type=jnp.float32
    )
    grad_values = grad_values.reshape(local_frames, width_heads).astype(jnp.bfloat16)
    grad_normed = (
        dot_against(grad_queries, q_weight)
        + dot_against(grad_keys, k_weight)
        + dot_against(grad_values, v_weight)
    )
    grad_mean = jnp.mean(grad_normed, axis=-1, keepdims=True)
    grad_along = jnp.mean(grad_normed * normed_f, axis=-1, keepdims=True)
    grad_rows = grad_frames.astype(jnp.float32) + inverse * (
        grad_normed - grad_mean - normed_f * grad_along
    )
    grad_rows = grad_rows.astype(jnp.bfloat16)
    shares = lax.psum_scatter(
        jnp.concatenate(
            [
                dot_across(normed, grad_queries),
                dot_across(normed, grad_keys),
                dot_across(normed, grad_values),
                dot_across(grad_frames, context),
            ],
            axis=1,
        ).astype(jnp.bfloat16),
        "fsdp",
        scatter_dimension=0,
        tiled=True,
    ).astype(jnp.float32)
    totals = lax.psum(shares, ("dp", "seq"))
    token_count = (
        signal.shape[0]
        * lax.axis_size("dp")
        * lax.axis_size("fsdp")
        * local_frames
        * lax.axis_size("seq")
    )
    totals = totals * token_count ** (-0.5)
    return (
        output_rows[None],
        grad_rows[None],
        totals[:, :width_heads],
        totals[:, width_heads : 2 * width_heads],
        totals[:, 2 * width_heads : 3 * width_heads],
        totals[:, 3 * width_heads :],
    )


F32 = jnp.float32
BF16 = jnp.bfloat16
MESH = pl.DeviceIdType.MESH
N_SEMS = 38


def rows_of(index, size):
    return pl.ds(pl.multiple_of(index * size, size), size)


def fused_kernel(
    token_count,
    sig_ref, up_ref, wq_ref, wk_ref, wv_ref, wo_ref,
    out_ref, gsig_ref, gq_ref, gk_ref, gv_ref, go_ref,
    weights, sig_all, up_all, normed, qkv, gctx, ctx, grads3,
    partial, landed, summed, landed_z, final,
    out_send, out_recv, gn_send, gn_recv, send_sems, recv_sems,
):
    dp, core, z = lax.axis_index("dp"), lax.axis_index("seq"), lax.axis_index("fsdp")
    n_dp, n_z = lax.axis_size("dp"), lax.axis_size("fsdp")
    half = wq_ref.shape[1] // 2
    block = wq_ref.shape[0]
    piece = block // n_dp
    frames = sig_ref.shape[0]
    scale = HSIZE ** (-0.5)

    def copy(src, dst, sem, axis, to):
        return pltpu.make_async_remote_copy(
            src_ref=src, dst_ref=dst, send_sem=send_sems.at[sem], recv_sem=recv_sems.at[sem],
            device_id={axis: to}, device_id_type=MESH,
        )

    def forth(index, step, size):
        return lax.rem(index + step, size)

    def back(index, step, size):
        return lax.rem(index + size - step, size)

    barrier = pltpu.get_barrier_semaphore()
    for step in range(1, n_dp):
        pl.semaphore_signal(barrier, inc=1, device_id={"dp": forth(dp, step, n_dp)}, device_id_type=MESH)
    for step in range(1, n_z):
        pl.semaphore_signal(barrier, inc=1, device_id={"fsdp": forth(z, step, n_z)}, device_id_type=MESH)
    pl.semaphore_signal(barrier, inc=1, device_id={"seq": 1 - core}, device_id_type=MESH)

    own_cols = pl.ds(pl.multiple_of(core * half, half), half)
    own_block = rows_of(z, block)
    for at, ref in enumerate((wq_ref, wk_ref, wv_ref, wo_ref)):
        weights[own_block, at * half : (at + 1) * half] = ref[:, own_cols]
    pl.semaphore_wait(barrier, n_dp + n_z - 1)

    sends = []

    def start(*args):
        one = copy(*args)
        one.start()
        sends.append(one)

    def arrived(dst, sem):
        copy(dst, dst, sem, "seq", 1 - core).wait_recv()

    def weight_rows(shard, quarter):
        return weights.at[pl.ds(pl.multiple_of(shard * block + quarter * piece, piece), piece)]

    mine = weight_rows(z, dp)
    for step in (1, 2, 3):
        start(mine, mine, step - 1, "fsdp", forth(z, step, n_z))
    own_frames = rows_of(core, frames)
    far_frames = rows_of(1 - core, frames)
    start(sig_ref, sig_all.at[own_frames], 12, "seq", 1 - core)
    start(up_ref, up_all.at[own_frames], 13, "seq", 1 - core)
    normed_f, inverse = normalize(sig_ref[...])
    normed[own_frames, :] = normed_f.astype(BF16)
    up_all[own_frames, :] = up_ref[...]
    arrived(sig_all.at[far_frames], 12)
    far_normed, _ = normalize(sig_all[far_frames, :])
    normed[far_frames, :] = far_normed.astype(BF16)
    arrived(up_all.at[far_frames], 13)

    for step in (1, 2, 3):
        source = back(z, step, n_z)
        held = weight_rows(source, dp)
        arrived(held, step - 1)
        for peer in (1, 2, 3):
            start(held, held, 3 + (step - 1) * 3 + peer - 1, "dp", forth(dp, peer, n_dp))

    for step in (0, 1, 2, 3):
        source = back(z, step, n_z)
        if step:
            for peer in (1, 2, 3):
                arrived(weight_rows(source, back(dp, peer, n_dp)), 3 + (step - 1) * 3 + peer - 1)
        rows = rows_of(source, block)
        first = jnp.dot(normed[:, rows], weights[rows, : 3 * half], preferred_element_type=F32)
        second = jnp.dot(up_all[:, rows], weights[rows, 3 * half :], preferred_element_type=F32)
        if step:
            first = qkv[...] + first
            second = gctx[...] + second
        qkv[...] = first
        gctx[...] = second

    for head in range(half // HSIZE):
        cols = slice(head * HSIZE, (head + 1) * HSIZE)
        query = qkv[:, head * HSIZE : (head + 1) * HSIZE].astype(BF16)
        key = qkv[:, half + head * HSIZE : half + (head + 1) * HSIZE].astype(BF16)
        value = qkv[:, 2 * half + head * HSIZE : 2 * half + (head + 1) * HSIZE].astype(BF16)
        grad = gctx[:, cols].astype(BF16)
        scores = dot_against(query, key) * scale
        exponent = jnp.exp(scores - jnp.max(scores, axis=-1, keepdims=True))
        attention = exponent / jnp.sum(exponent, axis=-1, keepdims=True)
        attn_weights = attention.astype(BF16)
        ctx[:, cols] = jnp.dot(attn_weights, value, preferred_element_type=F32).astype(BF16)
        grad_attention = dot_against(grad, value)
        delta = jnp.sum(attention * grad_attention, axis=-1, keepdims=True)
        grad_scores = (attention * (grad_attention - delta) * scale).astype(BF16)
        grads3[:, cols] = jnp.dot(grad_scores, key, preferred_element_type=F32).astype(BF16)
        grads3[:, half + head * HSIZE : half + (head + 1) * HSIZE] = dot_across(
            grad_scores, query
        ).astype(BF16)
        grads3[:, 2 * half + head * HSIZE : 2 * half + (head + 1) * HSIZE] = dot_across(
            attn_weights, grad
        ).astype(BF16)

    order = (2, 1, 3, 0)
    for step in order:
        cols = rows_of(forth(z, step, n_z), block)
        partial[step, :, : 3 * half] = dot_across(normed[:, cols], grads3[...]).astype(BF16)
        partial[step, :, 3 * half :] = dot_across(up_all[:, cols], ctx[...]).astype(BF16)
        for peer in (1, 2, 3):
            to = forth(dp, peer, n_dp)
            start(
                partial.at[step, rows_of(to, piece)], landed.at[step, peer - 1],
                14 + step * 3 + peer - 1, "dp", to,
            )

    out_send[...] = dot_against(ctx[far_frames, :], weights[:, 3 * half :])
    start(out_send, out_recv, 26, "seq", 1 - core)
    gn_send[...] = dot_against(grads3[far_frames, :], weights[:, : 3 * half])
    start(gn_send, gn_recv, 27, "seq", 1 - core)
    out_own = dot_against(ctx[own_frames, :], weights[:, 3 * half :])
    arrived(out_recv, 26)
    out_ref[...] = (sig_ref[...].astype(F32) + (out_own + out_recv[...])).astype(BF16)

    for step in order:
        for peer in (1, 2, 3):
            arrived(landed.at[step, peer - 1], 14 + step * 3 + peer - 1)
        total = partial[step, rows_of(dp, piece), :].astype(F32)
        for peer in (1, 2, 3):
            total = total + landed[step, peer - 1].astype(F32)
        summed[step] = total.astype(BF16)
        if step:
            start(summed.at[step], landed_z.at[step - 1], 28 + step - 1, "fsdp", forth(z, step, n_z))

    gn_own = dot_against(grads3[own_frames, :], weights[:, : 3 * half])
    arrived(gn_recv, 27)
    grad_normed = gn_own + gn_recv[...]
    normed_f, inverse = normalize(sig_ref[...])
    grad_mean = jnp.mean(grad_normed, axis=-1, keepdims=True)
    grad_along = jnp.mean(grad_normed * normed_f, axis=-1, keepdims=True)
    gsig_ref[...] = (
        up_ref[...].astype(F32) + inverse * (grad_normed - grad_mean - normed_f * grad_along)
    ).astype(BF16)

    total = summed[0].astype(F32)
    for step in (1, 2, 3):
        arrived(landed_z.at[step - 1], 28 + step - 1)
        total = total + landed_z[step - 1].astype(F32)
    own_piece = rows_of(dp, piece)
    final[core, own_piece, :] = total.astype(BF16)
    place = final.at[core, own_piece]
    for peer in (1, 2, 3):
        start(place, place, 31 + peer - 1, "dp", forth(dp, peer, n_dp))
    start(place, place, 34, "seq", 1 - core)
    for peer in (1, 2, 3):
        place = final.at[core, rows_of(back(dp, peer, n_dp), piece)]
        arrived(place, 31 + peer - 1)
        start(place, place, 34 + peer, "seq", 1 - core)
    for peer in (0, 1, 2, 3):
        arrived(final.at[1 - core, rows_of(back(dp, peer, n_dp), piece)], 34 + peer)

    factor = token_count ** (-0.5)
    for at, ref in enumerate((gq_ref, gk_ref, gv_ref, go_ref)):
        for side in (0, 1):
            ref[:, side * half : (side + 1) * half] = (
                final[side, :, at * half : (at + 1) * half].astype(F32) * factor
            )
    for one in sends:
        one.wait_send()


def fused_body(signal, w_query, w_key, w_value, w_output, upstream):
    frames, width = signal.shape[1:]
    block, heads_width = w_query.shape
    both, half = 2 * frames, heads_width // 2
    n_dp, n_z = lax.axis_size("dp"), lax.axis_size("fsdp")
    piece = block // n_dp
    token_count = signal.shape[0] * n_dp * n_z * both
    vmem = pl.BlockSpec(memory_space=pltpu.VMEM)
    rows_shape = jax.ShapeDtypeStruct((frames, width), BF16)
    grad_shape = jax.ShapeDtypeStruct((block, heads_width), F32)

    def kernel(*refs):
        fused_kernel(token_count, *refs)

    output_rows, grad_rows, *grads = pl.pallas_call(
        kernel,
        out_shape=[rows_shape, rows_shape] + [grad_shape] * 4,
        in_specs=[vmem] * 6,
        out_specs=[vmem] * 6,
        scratch_shapes=[
            pltpu.VMEM((width, 4 * half), BF16),
            pltpu.VMEM((both, width), BF16),
            pltpu.VMEM((both, width), BF16),
            pltpu.VMEM((both, width), BF16),
            pltpu.VMEM((both, 3 * half), F32),
            pltpu.VMEM((both, half), F32),
            pltpu.VMEM((both, half), BF16),
            pltpu.VMEM((both, 3 * half), BF16),
            pltpu.VMEM((n_z, block, 4 * half), BF16),
            pltpu.VMEM((n_z, n_dp - 1, piece, 4 * half), BF16),
            pltpu.VMEM((n_z, piece, 4 * half), BF16),
            pltpu.VMEM((n_z - 1, piece, 4 * half), BF16),
            pltpu.VMEM((2, block, 4 * half), BF16),
            pltpu.VMEM((frames, width), F32),
            pltpu.VMEM((frames, width), F32),
            pltpu.VMEM((frames, width), F32),
            pltpu.VMEM((frames, width), F32),
            pltpu.SemaphoreType.DMA((N_SEMS,)),
            pltpu.SemaphoreType.DMA((N_SEMS,)),
        ],
        compiler_params=pltpu.CompilerParams(
            collective_id=0, has_side_effects=True, vmem_limit_bytes=44 * 1024 * 1024
        ),
    )(signal[0], upstream[0], w_query, w_key, w_value, w_output)
    return (output_rows[None], grad_rows[None], *grads)


def fits(mesh):
    return mesh.shape["dp"] == 4 and mesh.shape["seq"] == 2 and mesh.shape["fsdp"] == 4


def solution(mesh):
    placed = (
        P(("dp", "fsdp"), "seq", None),
        P("fsdp", None),
        P("fsdp", None),
        P("fsdp", None),
        P("fsdp", None),
        P(("dp", "fsdp"), "seq", None),
    )
    return jax.shard_map(
        fused_body if fits(mesh) else body,
        mesh=mesh,
        in_specs=placed,
        out_specs=(
            P(("dp", "fsdp"), "seq", None),
            P(("dp", "fsdp"), "seq", None),
            P("fsdp", None),
            P("fsdp", None),
            P("fsdp", None),
            P("fsdp", None),
        ),
        check_vma=False,
    )
```

```python
import jax
import jax.numpy as jnp
from jax import lax
from jax.experimental import pallas as pl
from jax.experimental.pallas import tpu as pltpu
from jax.sharding import PartitionSpec as P

HEADS = 8
HSIZE = 64


def normalize(frame_rows):
    widened = frame_rows.astype(jnp.float32)
    centre = widened - jnp.mean(widened, axis=-1, keepdims=True)
    variance = jnp.mean(centre * centre, axis=-1, keepdims=True)
    inverse = lax.rsqrt(variance + 1e-05)
    return (centre * inverse, inverse)


def split_heads(matrix):
    return matrix.reshape(matrix.shape[0], HEADS, HSIZE)


def dot_across(left, right):
    return lax.dot_general(
        left, right, (((0,), (0,)), ((), ())), preferred_element_type=jnp.float32
    )


def dot_against(left, right):
    return lax.dot_general(
        left, right, (((1,), (1,)), ((), ())), preferred_element_type=jnp.float32
    )


def body(signal, w_query, w_key, w_value, w_output, upstream):
    q_weight, k_weight, v_weight, o_weight = (
        lax.all_gather(w_query, "fsdp", axis=0, tiled=True),
        lax.all_gather(w_key, "fsdp", axis=0, tiled=True),
        lax.all_gather(w_value, "fsdp", axis=0, tiled=True),
        lax.all_gather(w_output, "fsdp", axis=0, tiled=True),
    )
    score_scale = HSIZE ** (-0.5)
    frame_rows = signal[0]
    grad_frames = upstream[0]
    local_frames = frame_rows.shape[0]
    width_heads = q_weight.shape[1]
    normed_f, inverse = normalize(frame_rows)
    normed = normed_f.astype(jnp.bfloat16)
    queries = jnp.dot(normed, q_weight, preferred_element_type=jnp.float32).astype(jnp.bfloat16)
    key_rows = jnp.dot(normed, k_weight, preferred_element_type=jnp.float32).astype(jnp.bfloat16)
    value_rows = jnp.dot(normed, v_weight, preferred_element_type=jnp.float32).astype(jnp.bfloat16)
    all_keys, all_values = (
        lax.all_gather(key_rows, "seq", axis=0, tiled=True),
        lax.all_gather(value_rows, "seq", axis=0, tiled=True),
    )
    query_heads = split_heads(queries)
    key_heads = split_heads(all_keys)
    value_heads = split_heads(all_values)
    scores = (
        jnp.einsum("qhs,khs->hqk", query_heads, key_heads, preferred_element_type=jnp.float32)
        * score_scale
    )
    row_max = jnp.max(scores, axis=-1, keepdims=True)
    exponent = jnp.exp(scores - row_max)
    row_total = jnp.sum(exponent, axis=-1, keepdims=True)
    attention = exponent / row_total
    attn_weights = attention.astype(jnp.bfloat16)
    context = jnp.einsum(
        "hqk,khs->qhs", attn_weights, value_heads, preferred_element_type=jnp.float32
    )
    context = context.reshape(local_frames, width_heads).astype(jnp.bfloat16)
    projected = dot_against(context, o_weight)
    output_rows = (frame_rows.astype(jnp.float32) + projected).astype(jnp.bfloat16)
    grad_context = jnp.dot(grad_frames, o_weight, preferred_element_type=jnp.float32).astype(
        jnp.bfloat16
    )
    grad_heads = split_heads(grad_context)
    grad_attention = jnp.einsum(
        "qhs,khs->hqk", grad_heads, value_heads, preferred_element_type=jnp.float32
    )
    row_delta = jnp.sum(attention * grad_attention, axis=-1, keepdims=True)
    grad_scores = (attention * (grad_attention - row_delta) * score_scale).astype(jnp.bfloat16)
    grad_queries = jnp.einsum(
        "hqk,khs->qhs", grad_scores, key_heads, preferred_element_type=jnp.float32
    )
    grad_queries = grad_queries.reshape(local_frames, width_heads).astype(jnp.bfloat16)
    all_queries, all_grad_context = (
        lax.all_gather(queries, "seq", axis=0, tiled=True),
        lax.all_gather(grad_context, "seq", axis=0, tiled=True),
    )
    all_max, all_total, all_delta = (
        lax.all_gather(row_max, "seq", axis=1, tiled=True),
        lax.all_gather(row_total, "seq", axis=1, tiled=True),
        lax.all_gather(row_delta, "seq", axis=1, tiled=True),
    )
    far_query_heads = split_heads(all_queries)
    far_grad_heads = split_heads(all_grad_context)
    own_keys = split_heads(key_rows)
    own_values = split_heads(value_rows)
    far_scores = (
        jnp.einsum("qhs,khs->hqk", far_query_heads, own_keys, preferred_element_type=jnp.float32)
        * score_scale
    )
    far_attention = jnp.exp(far_scores - all_max) / all_total
    far_weights = far_attention.astype(jnp.bfloat16)
    far_grad = jnp.einsum(
        "qhs,khs->hqk", far_grad_heads, own_values, preferred_element_type=jnp.float32
    )
    far_scaled = (far_attention * (far_grad - all_delta) * score_scale).astype(jnp.bfloat16)
    grad_keys = jnp.einsum(
        "hqk,qhs->khs", far_scaled, far_query_heads, preferred_element_type=jnp.float32
    )
    grad_keys = grad_keys.reshape(local_frames, width_heads).astype(jnp.bfloat16)
    grad_values = jnp.einsum(
        "hqk,qhs->khs", far_weights, far_grad_heads, preferred_element_type=jnp.float32
    )
    grad_values = grad_values.reshape(local_frames, width_heads).astype(jnp.bfloat16)
    grad_normed = (
        dot_against(grad_queries, q_weight)
        + dot_against(grad_keys, k_weight)
        + dot_against(grad_values, v_weight)
    )
    grad_mean = jnp.mean(grad_normed, axis=-1, keepdims=True)
    grad_along = jnp.mean(grad_normed * normed_f, axis=-1, keepdims=True)
    grad_rows = grad_frames.astype(jnp.float32) + inverse * (
        grad_normed - grad_mean - normed_f * grad_along
    )
    grad_rows = grad_rows.astype(jnp.bfloat16)
    shares = lax.psum_scatter(
        jnp.concatenate(
            [
                dot_across(normed, grad_queries),
                dot_across(normed, grad_keys),
                dot_across(normed, grad_values),
                dot_across(grad_frames, context),
            ],
            axis=1,
        ).astype(jnp.bfloat16),
        "fsdp",
        scatter_dimension=0,
        tiled=True,
    ).astype(jnp.float32)
    totals = lax.psum(shares, ("dp", "seq"))
    token_count = (
        signal.shape[0]
        * lax.axis_size("dp")
        * lax.axis_size("fsdp")
        * local_frames
        * lax.axis_size("seq")
    )
    totals = totals * token_count ** (-0.5)
    return (
        output_rows[None],
        grad_rows[None],
        totals[:, :width_heads],
        totals[:, width_heads : 2 * width_heads],
        totals[:, 2 * width_heads : 3 * width_heads],
        totals[:, 3 * width_heads :],
    )


F32 = jnp.float32
BF16 = jnp.bfloat16
MESH = pl.DeviceIdType.MESH
N_SEMS = 38


def rows_of(index, size):
    return pl.ds(pl.multiple_of(index * size, size), size)


def fused_kernel(
    token_count,
    rows_ref, w_ref,
    out_ref, gsig_ref, gq_ref, gk_ref, gv_ref, go_ref,
    weights, sig_all, up_all, normed, qkv, gctx, ctx, grads3,
    partial, landed, summed, landed_z, final,
    out_send, out_recv, gn_send, gn_recv, send_sems, recv_sems,
):
    block, frames = w_ref.shape[0] // 4, rows_ref.shape[0] // 2
    sig_ref, up_ref = (rows_ref.at[at * frames : (at + 1) * frames] for at in range(2))
    wq_ref, wk_ref, wv_ref, wo_ref = (w_ref.at[at * block : (at + 1) * block] for at in range(4))
    dp, core, z = lax.axis_index("dp"), lax.axis_index("seq"), lax.axis_index("fsdp")
    n_dp, n_z = lax.axis_size("dp"), lax.axis_size("fsdp")
    half = wq_ref.shape[1] // 2
    piece = block // n_dp
    scale = HSIZE ** (-0.5)

    def copy(src, dst, sem, axis, to):
        return pltpu.make_async_remote_copy(
            src_ref=src, dst_ref=dst, send_sem=send_sems.at[sem], recv_sem=recv_sems.at[sem],
            device_id={axis: to}, device_id_type=MESH,
        )

    def forth(index, step, size):
        return lax.rem(index + step, size)

    def back(index, step, size):
        return lax.rem(index + size - step, size)

    barrier = pltpu.get_barrier_semaphore()
    for step in range(1, n_dp):
        pl.semaphore_signal(barrier, inc=1, device_id={"dp": forth(dp, step, n_dp)}, device_id_type=MESH)
    for step in range(1, n_z):
        pl.semaphore_signal(barrier, inc=1, device_id={"fsdp": forth(z, step, n_z)}, device_id_type=MESH)
    pl.semaphore_signal(barrier, inc=1, device_id={"seq": 1 - core}, device_id_type=MESH)

    own_cols = pl.ds(pl.multiple_of(core * half, half), half)
    own_block = rows_of(z, block)
    for at, ref in enumerate((wq_ref, wk_ref, wv_ref, wo_ref)):
        weights[own_block, at * half : (at + 1) * half] = ref[:, own_cols]
    pl.semaphore_wait(barrier, n_dp + n_z - 1)

    sends = []

    def start(*args):
        one = copy(*args)
        one.start()
        sends.append(one)

    def arrived(dst, sem):
        copy(dst, dst, sem, "seq", 1 - core).wait_recv()

    def weight_rows(shard, quarter):
        return weights.at[pl.ds(pl.multiple_of(shard * block + quarter * piece, piece), piece)]

    mine = weight_rows(z, dp)
    for step in (1, 2, 3):
        start(mine, mine, step - 1, "fsdp", forth(z, step, n_z))
    own_frames = rows_of(core, frames)
    far_frames = rows_of(1 - core, frames)
    start(sig_ref, sig_all.at[own_frames], 12, "seq", 1 - core)
    start(up_ref, up_all.at[own_frames], 13, "seq", 1 - core)
    normed_f, inverse = normalize(sig_ref[...])
    normed[own_frames, :] = normed_f.astype(BF16)
    up_all[own_frames, :] = up_ref[...]
    arrived(sig_all.at[far_frames], 12)
    far_normed, _ = normalize(sig_all[far_frames, :])
    normed[far_frames, :] = far_normed.astype(BF16)
    arrived(up_all.at[far_frames], 13)

    for step in (1, 2, 3):
        source = back(z, step, n_z)
        held = weight_rows(source, dp)
        arrived(held, step - 1)
        for peer in (1, 2, 3):
            start(held, held, 3 + (step - 1) * 3 + peer - 1, "dp", forth(dp, peer, n_dp))

    for step in (0, 1, 2, 3):
        source = back(z, step, n_z)
        if step:
            for peer in (1, 2, 3):
                arrived(weight_rows(source, back(dp, peer, n_dp)), 3 + (step - 1) * 3 + peer - 1)
        rows = rows_of(source, block)
        first = jnp.dot(normed[:, rows], weights[rows, : 3 * half], preferred_element_type=F32)
        second = jnp.dot(up_all[:, rows], weights[rows, 3 * half :], preferred_element_type=F32)
        if step:
            first = qkv[...] + first
            second = gctx[...] + second
        qkv[...] = first
        gctx[...] = second

    for head in range(half // HSIZE):
        cols = slice(head * HSIZE, (head + 1) * HSIZE)
        query = qkv[:, head * HSIZE : (head + 1) * HSIZE].astype(BF16)
        key = qkv[:, half + head * HSIZE : half + (head + 1) * HSIZE].astype(BF16)
        value = qkv[:, 2 * half + head * HSIZE : 2 * half + (head + 1) * HSIZE].astype(BF16)
        grad = gctx[:, cols].astype(BF16)
        scores = dot_against(query, key) * scale
        exponent = jnp.exp(scores - jnp.max(scores, axis=-1, keepdims=True))
        attention = exponent / jnp.sum(exponent, axis=-1, keepdims=True)
        attn_weights = attention.astype(BF16)
        ctx[:, cols] = jnp.dot(attn_weights, value, preferred_element_type=F32).astype(BF16)
        grad_attention = dot_against(grad, value)
        delta = jnp.sum(attention * grad_attention, axis=-1, keepdims=True)
        grad_scores = (attention * (grad_attention - delta) * scale).astype(BF16)
        grads3[:, cols] = jnp.dot(grad_scores, key, preferred_element_type=F32).astype(BF16)
        grads3[:, half + head * HSIZE : half + (head + 1) * HSIZE] = dot_across(
            grad_scores, query
        ).astype(BF16)
        grads3[:, 2 * half + head * HSIZE : 2 * half + (head + 1) * HSIZE] = dot_across(
            attn_weights, grad
        ).astype(BF16)

    order = (2, 1, 3, 0)
    for step in order:
        cols = rows_of(forth(z, step, n_z), block)
        partial[step, :, : 3 * half] = dot_across(normed[:, cols], grads3[...]).astype(BF16)
        partial[step, :, 3 * half :] = dot_across(up_all[:, cols], ctx[...]).astype(BF16)
        for peer in (1, 2, 3):
            to = forth(dp, peer, n_dp)
            start(
                partial.at[step, rows_of(to, piece)], landed.at[step, peer - 1],
                14 + step * 3 + peer - 1, "dp", to,
            )

    out_send[...] = dot_against(ctx[far_frames, :], weights[:, 3 * half :])
    start(out_send, out_recv, 26, "seq", 1 - core)
    gn_send[...] = dot_against(grads3[far_frames, :], weights[:, : 3 * half])
    start(gn_send, gn_recv, 27, "seq", 1 - core)
    out_own = dot_against(ctx[own_frames, :], weights[:, 3 * half :])
    arrived(out_recv, 26)
    out_ref[...] = (sig_ref[...].astype(F32) + (out_own + out_recv[...])).astype(BF16)

    for step in order:
        for peer in (1, 2, 3):
            arrived(landed.at[step, peer - 1], 14 + step * 3 + peer - 1)
        total = partial[step, rows_of(dp, piece), :].astype(F32)
        for peer in (1, 2, 3):
            total = total + landed[step, peer - 1].astype(F32)
        summed[step] = total.astype(BF16)
        if step:
            start(summed.at[step], landed_z.at[step - 1], 28 + step - 1, "fsdp", forth(z, step, n_z))

    gn_own = dot_against(grads3[own_frames, :], weights[:, : 3 * half])
    arrived(gn_recv, 27)
    grad_normed = gn_own + gn_recv[...]
    normed_f, inverse = normalize(sig_ref[...])
    grad_mean = jnp.mean(grad_normed, axis=-1, keepdims=True)
    grad_along = jnp.mean(grad_normed * normed_f, axis=-1, keepdims=True)
    gsig_ref[...] = (
        up_ref[...].astype(F32) + inverse * (grad_normed - grad_mean - normed_f * grad_along)
    ).astype(BF16)

    total = summed[0].astype(F32)
    for step in (1, 2, 3):
        arrived(landed_z.at[step - 1], 28 + step - 1)
        total = total + landed_z[step - 1].astype(F32)
    own_piece = rows_of(dp, piece)
    final[core, own_piece, :] = total.astype(BF16)
    place = final.at[core, own_piece]
    for peer in (1, 2, 3):
        start(place, place, 31 + peer - 1, "dp", forth(dp, peer, n_dp))
    start(place, place, 34, "seq", 1 - core)
    for peer in (1, 2, 3):
        place = final.at[core, rows_of(back(dp, peer, n_dp), piece)]
        arrived(place, 31 + peer - 1)
        start(place, place, 34 + peer, "seq", 1 - core)
    for peer in (0, 1, 2, 3):
        arrived(final.at[1 - core, rows_of(back(dp, peer, n_dp), piece)], 34 + peer)

    factor = token_count ** (-0.5)
    for at, ref in enumerate((gq_ref, gk_ref, gv_ref, go_ref)):
        for side in (0, 1):
            ref[:, side * half : (side + 1) * half] = (
                final[side, :, at * half : (at + 1) * half].astype(F32) * factor
            )
    for one in sends:
        one.wait_send()


def fused_body(signal, w_query, w_key, w_value, w_output, upstream):
    frames, width = signal.shape[1:]
    block, heads_width = w_query.shape
    both, half = 2 * frames, heads_width // 2
    n_dp, n_z = lax.axis_size("dp"), lax.axis_size("fsdp")
    piece = block // n_dp
    token_count = signal.shape[0] * n_dp * n_z * both
    vmem = pl.BlockSpec(memory_space=pltpu.VMEM)
    rows_shape = jax.ShapeDtypeStruct((frames, width), BF16)
    grad_shape = jax.ShapeDtypeStruct((block, heads_width), F32)

    def kernel(*refs):
        fused_kernel(token_count, *refs)

    output_rows, grad_rows, *grads = pl.pallas_call(
        kernel,
        out_shape=[rows_shape, rows_shape] + [grad_shape] * 4,
        in_specs=[vmem] * 2,
        out_specs=[vmem] * 6,
        scratch_shapes=[
            pltpu.VMEM((width, 4 * half), BF16),
            pltpu.VMEM((both, width), BF16),
            pltpu.VMEM((both, width), BF16),
            pltpu.VMEM((both, width), BF16),
            pltpu.VMEM((both, 3 * half), F32),
            pltpu.VMEM((both, half), F32),
            pltpu.VMEM((both, half), BF16),
            pltpu.VMEM((both, 3 * half), BF16),
            pltpu.VMEM((n_z, block, 4 * half), BF16),
            pltpu.VMEM((n_z, n_dp - 1, piece, 4 * half), BF16),
            pltpu.VMEM((n_z, piece, 4 * half), BF16),
            pltpu.VMEM((n_z - 1, piece, 4 * half), BF16),
            pltpu.VMEM((2, block, 4 * half), BF16),
            pltpu.VMEM((frames, width), F32),
            pltpu.VMEM((frames, width), F32),
            pltpu.VMEM((frames, width), F32),
            pltpu.VMEM((frames, width), F32),
            pltpu.SemaphoreType.DMA((N_SEMS,)),
            pltpu.SemaphoreType.DMA((N_SEMS,)),
        ],
        compiler_params=pltpu.CompilerParams(
            collective_id=0, has_side_effects=True, vmem_limit_bytes=44 * 1024 * 1024
        ),
    )(
        jnp.concatenate([signal[0], upstream[0]], axis=0),
        jnp.concatenate([w_query, w_key, w_value, w_output], axis=0),
    )
    return (output_rows[None], grad_rows[None], *grads)


def fits(mesh):
    return mesh.shape["dp"] == 4 and mesh.shape["seq"] == 2 and mesh.shape["fsdp"] == 4


def solution(mesh):
    placed = (
        P(("dp", "fsdp"), "seq", None),
        P("fsdp", None),
        P("fsdp", None),
        P("fsdp", None),
        P("fsdp", None),
        P(("dp", "fsdp"), "seq", None),
    )
    return jax.shard_map(
        fused_body if fits(mesh) else body,
        mesh=mesh,
        in_specs=placed,
        out_specs=(
            P(("dp", "fsdp"), "seq", None),
            P(("dp", "fsdp"), "seq", None),
            P("fsdp", None),
            P("fsdp", None),
            P("fsdp", None),
            P("fsdp", None),
        ),
        check_vma=False,
    )
```

```python
import jax
import jax.numpy as jnp
from jax import lax
from jax.experimental import pallas as pl
from jax.experimental.pallas import tpu as pltpu
from jax.sharding import PartitionSpec as P

HEADS = 8
HSIZE = 64


def normalize(frame_rows):
    widened = frame_rows.astype(jnp.float32)
    centre = widened - jnp.mean(widened, axis=-1, keepdims=True)
    variance = jnp.mean(centre * centre, axis=-1, keepdims=True)
    inverse = lax.rsqrt(variance + 1e-05)
    return (centre * inverse, inverse)


def split_heads(matrix):
    return matrix.reshape(matrix.shape[0], HEADS, HSIZE)


def dot_across(left, right):
    return lax.dot_general(
        left, right, (((0,), (0,)), ((), ())), preferred_element_type=jnp.float32
    )


def dot_against(left, right):
    return lax.dot_general(
        left, right, (((1,), (1,)), ((), ())), preferred_element_type=jnp.float32
    )


def body(signal, w_query, w_key, w_value, w_output, upstream):
    q_weight, k_weight, v_weight, o_weight = (
        lax.all_gather(w_query, "fsdp", axis=0, tiled=True),
        lax.all_gather(w_key, "fsdp", axis=0, tiled=True),
        lax.all_gather(w_value, "fsdp", axis=0, tiled=True),
        lax.all_gather(w_output, "fsdp", axis=0, tiled=True),
    )
    score_scale = HSIZE ** (-0.5)
    frame_rows = signal[0]
    grad_frames = upstream[0]
    local_frames = frame_rows.shape[0]
    width_heads = q_weight.shape[1]
    normed_f, inverse = normalize(frame_rows)
    normed = normed_f.astype(jnp.bfloat16)
    queries = jnp.dot(normed, q_weight, preferred_element_type=jnp.float32).astype(jnp.bfloat16)
    key_rows = jnp.dot(normed, k_weight, preferred_element_type=jnp.float32).astype(jnp.bfloat16)
    value_rows = jnp.dot(normed, v_weight, preferred_element_type=jnp.float32).astype(jnp.bfloat16)
    all_keys, all_values = (
        lax.all_gather(key_rows, "seq", axis=0, tiled=True),
        lax.all_gather(value_rows, "seq", axis=0, tiled=True),
    )
    query_heads = split_heads(queries)
    key_heads = split_heads(all_keys)
    value_heads = split_heads(all_values)
    scores = (
        jnp.einsum("qhs,khs->hqk", query_heads, key_heads, preferred_element_type=jnp.float32)
        * score_scale
    )
    row_max = jnp.max(scores, axis=-1, keepdims=True)
    exponent = jnp.exp(scores - row_max)
    row_total = jnp.sum(exponent, axis=-1, keepdims=True)
    attention = exponent / row_total
    attn_weights = attention.astype(jnp.bfloat16)
    context = jnp.einsum(
        "hqk,khs->qhs", attn_weights, value_heads, preferred_element_type=jnp.float32
    )
    context = context.reshape(local_frames, width_heads).astype(jnp.bfloat16)
    projected = dot_against(context, o_weight)
    output_rows = (frame_rows.astype(jnp.float32) + projected).astype(jnp.bfloat16)
    grad_context = jnp.dot(grad_frames, o_weight, preferred_element_type=jnp.float32).astype(
        jnp.bfloat16
    )
    grad_heads = split_heads(grad_context)
    grad_attention = jnp.einsum(
        "qhs,khs->hqk", grad_heads, value_heads, preferred_element_type=jnp.float32
    )
    row_delta = jnp.sum(attention * grad_attention, axis=-1, keepdims=True)
    grad_scores = (attention * (grad_attention - row_delta) * score_scale).astype(jnp.bfloat16)
    grad_queries = jnp.einsum(
        "hqk,khs->qhs", grad_scores, key_heads, preferred_element_type=jnp.float32
    )
    grad_queries = grad_queries.reshape(local_frames, width_heads).astype(jnp.bfloat16)
    all_queries, all_grad_context = (
        lax.all_gather(queries, "seq", axis=0, tiled=True),
        lax.all_gather(grad_context, "seq", axis=0, tiled=True),
    )
    all_max, all_total, all_delta = (
        lax.all_gather(row_max, "seq", axis=1, tiled=True),
        lax.all_gather(row_total, "seq", axis=1, tiled=True),
        lax.all_gather(row_delta, "seq", axis=1, tiled=True),
    )
    far_query_heads = split_heads(all_queries)
    far_grad_heads = split_heads(all_grad_context)
    own_keys = split_heads(key_rows)
    own_values = split_heads(value_rows)
    far_scores = (
        jnp.einsum("qhs,khs->hqk", far_query_heads, own_keys, preferred_element_type=jnp.float32)
        * score_scale
    )
    far_attention = jnp.exp(far_scores - all_max) / all_total
    far_weights = far_attention.astype(jnp.bfloat16)
    far_grad = jnp.einsum(
        "qhs,khs->hqk", far_grad_heads, own_values, preferred_element_type=jnp.float32
    )
    far_scaled = (far_attention * (far_grad - all_delta) * score_scale).astype(jnp.bfloat16)
    grad_keys = jnp.einsum(
        "hqk,qhs->khs", far_scaled, far_query_heads, preferred_element_type=jnp.float32
    )
    grad_keys = grad_keys.reshape(local_frames, width_heads).astype(jnp.bfloat16)
    grad_values = jnp.einsum(
        "hqk,qhs->khs", far_weights, far_grad_heads, preferred_element_type=jnp.float32
    )
    grad_values = grad_values.reshape(local_frames, width_heads).astype(jnp.bfloat16)
    grad_normed = (
        dot_against(grad_queries, q_weight)
        + dot_against(grad_keys, k_weight)
        + dot_against(grad_values, v_weight)
    )
    grad_mean = jnp.mean(grad_normed, axis=-1, keepdims=True)
    grad_along = jnp.mean(grad_normed * normed_f, axis=-1, keepdims=True)
    grad_rows = grad_frames.astype(jnp.float32) + inverse * (
        grad_normed - grad_mean - normed_f * grad_along
    )
    grad_rows = grad_rows.astype(jnp.bfloat16)
    shares = lax.psum_scatter(
        jnp.concatenate(
            [
                dot_across(normed, grad_queries),
                dot_across(normed, grad_keys),
                dot_across(normed, grad_values),
                dot_across(grad_frames, context),
            ],
            axis=1,
        ).astype(jnp.bfloat16),
        "fsdp",
        scatter_dimension=0,
        tiled=True,
    ).astype(jnp.float32)
    totals = lax.psum(shares, ("dp", "seq"))
    token_count = (
        signal.shape[0]
        * lax.axis_size("dp")
        * lax.axis_size("fsdp")
        * local_frames
        * lax.axis_size("seq")
    )
    totals = totals * token_count ** (-0.5)
    return (
        output_rows[None],
        grad_rows[None],
        totals[:, :width_heads],
        totals[:, width_heads : 2 * width_heads],
        totals[:, 2 * width_heads : 3 * width_heads],
        totals[:, 3 * width_heads :],
    )


F32 = jnp.float32
BF16 = jnp.bfloat16
MESH = pl.DeviceIdType.MESH
N_SEMS = 72


def rows_of(index, size):
    return pl.ds(pl.multiple_of(index * size, size), size)


def fused_kernel(
    token_count,
    rows_ref, w_ref,
    out_ref, gsig_ref, gq_ref, gk_ref, gv_ref, go_ref,
    weights, sig_all, up_all, normed, qkv, gctx, ctx, grads3,
    partial, relay_in, relay_out, landed, summed, landed_z, final,
    out_send, out_recv, gn_send, gn_recv, send_sems, recv_sems,
):
    block, frames = w_ref.shape[0] // 4, rows_ref.shape[0] // 2
    sig_ref, up_ref = (rows_ref.at[at * frames : (at + 1) * frames] for at in range(2))
    wq_ref, wk_ref, wv_ref, wo_ref = (w_ref.at[at * block : (at + 1) * block] for at in range(4))
    dp, core, z = lax.axis_index("dp"), lax.axis_index("seq"), lax.axis_index("fsdp")
    n_dp, n_z = lax.axis_size("dp"), lax.axis_size("fsdp")
    half = wq_ref.shape[1] // 2
    piece = block // n_dp
    scale = HSIZE ** (-0.5)

    slots = {}

    def copy(src, dst, name, axis, to):
        sem = slots.setdefault(name, len(slots))
        return pltpu.make_async_remote_copy(
            src_ref=src, dst_ref=dst, send_sem=send_sems.at[sem], recv_sem=recv_sems.at[sem],
            device_id={axis: to}, device_id_type=MESH,
        )

    def forth(index, step, size):
        return lax.rem(index + step, size)

    def back(index, step, size):
        return lax.rem(index + size - step, size)

    x_peer = dp + 1 - 2 * lax.rem(dp, 2)
    y_peer = lax.rem(dp + 2, n_dp)
    diagonal = n_dp - 1 - dp
    sibling = 1 - core
    barrier = pltpu.get_barrier_semaphore()
    for step in range(1, n_dp):
        pl.semaphore_signal(barrier, inc=1, device_id={"dp": forth(dp, step, n_dp)}, device_id_type=MESH)
    for step in range(1, n_z):
        pl.semaphore_signal(barrier, inc=1, device_id={"fsdp": forth(z, step, n_z)}, device_id_type=MESH)
    pl.semaphore_signal(barrier, inc=1, device_id={"seq": 1 - core}, device_id_type=MESH)

    own_cols = pl.ds(pl.multiple_of(core * half, half), half)
    own_block = rows_of(z, block)
    for at, ref in enumerate((wq_ref, wk_ref, wv_ref, wo_ref)):
        weights[own_block, at * half : (at + 1) * half] = ref[:, own_cols]
    pl.semaphore_wait(barrier, n_dp + n_z - 1)

    sends = []

    def start(*args):
        one = copy(*args)
        one.start()
        sends.append(one)

    def arrived(dst, name):
        copy(dst, dst, name, "seq", sibling).wait_recv()

    low, high = slice(0, piece // 2), slice(piece // 2, piece)
    half_piece = piece // 2

    def weight_rows(shard, quarter):
        return weights.at[pl.ds(pl.multiple_of(shard * block + quarter * piece, piece), piece)]

    def weight_half(shard, quarter, side):
        first = shard * block + quarter * piece + side * half_piece
        return weights.at[pl.ds(pl.multiple_of(first, half_piece), half_piece)]

    mine = weight_rows(z, dp)
    for step in (1, 2, 3):
        start(mine, mine, ("wz", step), "fsdp", forth(z, step, n_z))
    own_frames = rows_of(core, frames)
    far_frames = rows_of(1 - core, frames)
    start(sig_ref, sig_all.at[own_frames], "sig", "seq", 1 - core)
    start(up_ref, up_all.at[own_frames], "up", "seq", 1 - core)
    normed_f, inverse = normalize(sig_ref[...])
    normed[own_frames, :] = normed_f.astype(BF16)
    up_all[own_frames, :] = up_ref[...]
    arrived(sig_all.at[far_frames], "sig")
    far_normed, _ = normalize(sig_all[far_frames, :])
    normed[far_frames, :] = far_normed.astype(BF16)
    arrived(up_all.at[far_frames], "up")

    def spread(step):
        held = weight_rows(back(z, step, n_z), dp)
        arrived(held, ("wz", step))
        start(held, held, ("wx", step), "dp", x_peer)
        start(held, held, ("wy", step), "dp", y_peer)

    def pass_on(step):
        source = back(z, step, n_z)
        arrived(weight_rows(source, x_peer), ("wx", step))
        held = weight_half(source, x_peer, 0)
        start(held, held, ("wfy", step), "dp", y_peer)
        arrived(weight_rows(source, y_peer), ("wy", step))
        held = weight_half(source, y_peer, 1)
        start(held, held, ("wfx", step), "dp", x_peer)

    def project(step):
        source = back(z, step, n_z)
        if step:
            arrived(weight_half(source, diagonal, 0), ("wfy", step))
            arrived(weight_half(source, diagonal, 1), ("wfx", step))
        rows = rows_of(source, block)
        first = jnp.dot(normed[:, rows], weights[rows, : 3 * half], preferred_element_type=F32)
        second = jnp.dot(up_all[:, rows], weights[rows, 3 * half :], preferred_element_type=F32)
        if step:
            first = qkv[...] + first
            second = gctx[...] + second
        qkv[...] = first
        gctx[...] = second

    for step in (1, 2, 3):
        spread(step)
    project(0)
    for step in (1, 2, 3):
        pass_on(step)
    for step in (1, 2, 3):
        project(step)

    for head in range(half // HSIZE):
        cols = slice(head * HSIZE, (head + 1) * HSIZE)
        query = qkv[:, head * HSIZE : (head + 1) * HSIZE].astype(BF16)
        key = qkv[:, half + head * HSIZE : half + (head + 1) * HSIZE].astype(BF16)
        value = qkv[:, 2 * half + head * HSIZE : 2 * half + (head + 1) * HSIZE].astype(BF16)
        grad = gctx[:, cols].astype(BF16)
        scores = dot_against(query, key) * scale
        exponent = jnp.exp(scores - jnp.max(scores, axis=-1, keepdims=True))
        attention = exponent / jnp.sum(exponent, axis=-1, keepdims=True)
        attn_weights = attention.astype(BF16)
        ctx[:, cols] = jnp.dot(attn_weights, value, preferred_element_type=F32).astype(BF16)
        grad_attention = dot_against(grad, value)
        delta = jnp.sum(attention * grad_attention, axis=-1, keepdims=True)
        grad_scores = (attention * (grad_attention - delta) * scale).astype(BF16)
        grads3[:, cols] = jnp.dot(grad_scores, key, preferred_element_type=F32).astype(BF16)
        grads3[:, half + head * HSIZE : half + (head + 1) * HSIZE] = dot_across(
            grad_scores, query
        ).astype(BF16)
        grads3[:, 2 * half + head * HSIZE : 2 * half + (head + 1) * HSIZE] = dot_across(
            attn_weights, grad
        ).astype(BF16)

    order = (2, 1, 3, 0)

    def half_rows(step, quarter, side):
        first = quarter * piece + side * half_piece
        return partial.at[step, pl.ds(pl.multiple_of(first, half_piece), half_piece)]

    for step in order:
        cols = rows_of(forth(z, step, n_z), block)
        partial[step, :, : 3 * half] = dot_across(normed[:, cols], grads3[...]).astype(BF16)
        partial[step, :, 3 * half :] = dot_across(up_all[:, cols], ctx[...]).astype(BF16)
        for side, peer, name in ((0, x_peer, "x"), (1, y_peer, "y")):
            start(
                half_rows(step, diagonal, side), relay_in.at[step, side],
                ("relay" + name, step), "dp", peer,
            )
            start(
                half_rows(step, peer, side), landed.at[step, side, 0],
                ("near" + name, step), "dp", peer,
            )

    def relay(step):
        for side, peer, name in ((0, y_peer, "x"), (1, x_peer, "y")):
            arrived(relay_in.at[step, side], ("relay" + name, step))
            first = peer * piece + side * half_piece
            rows = pl.ds(pl.multiple_of(first, half_piece), half_piece)
            both = partial[step, rows, :].astype(F32) + relay_in[step, side].astype(F32)
            relay_out[step, side] = both.astype(BF16)
            start(
                relay_out.at[step, side], landed.at[step, side, 1],
                ("far" + name, step), "dp", peer,
            )

    relay(order[0])
    relay(order[1])
    out_send[...] = dot_against(ctx[far_frames, :], weights[:, 3 * half :])
    start(out_send, out_recv, "out", "seq", 1 - core)
    relay(order[2])
    gn_send[...] = dot_against(grads3[far_frames, :], weights[:, : 3 * half])
    start(gn_send, gn_recv, "gn", "seq", 1 - core)
    relay(order[3])
    out_own = dot_against(ctx[own_frames, :], weights[:, 3 * half :])
    arrived(out_recv, "out")
    out_ref[...] = (sig_ref[...].astype(F32) + (out_own + out_recv[...])).astype(BF16)

    for step in order:
        for side, name in ((0, "x"), (1, "y")):
            arrived(landed.at[step, side, 0], ("near" + name, step))
            arrived(landed.at[step, side, 1], ("far" + name, step))
            first = dp * piece + side * half_piece
            rows = pl.ds(pl.multiple_of(first, half_piece), half_piece)
            total = partial[step, rows, :].astype(F32)
            total = total + landed[step, side, 0].astype(F32) + landed[step, side, 1].astype(F32)
            summed[step, (low, high)[side], :] = total.astype(BF16)
        if step:
            start(summed.at[step], landed_z.at[step - 1], ("sz", step), "fsdp", forth(z, step, n_z))

    gn_own = dot_against(grads3[own_frames, :], weights[:, : 3 * half])
    arrived(gn_recv, "gn")
    grad_normed = gn_own + gn_recv[...]
    normed_f, inverse = normalize(sig_ref[...])
    grad_mean = jnp.mean(grad_normed, axis=-1, keepdims=True)
    grad_along = jnp.mean(grad_normed * normed_f, axis=-1, keepdims=True)
    gsig_ref[...] = (
        up_ref[...].astype(F32) + inverse * (grad_normed - grad_mean - normed_f * grad_along)
    ).astype(BF16)

    total = summed[0].astype(F32)
    for step in (1, 2, 3):
        arrived(landed_z.at[step - 1], ("sz", step))
        total = total + landed_z[step - 1].astype(F32)
    own_piece = rows_of(dp, piece)
    final[core, own_piece, :] = total.astype(BF16)
    def final_half(side_core, quarter, side):
        first = quarter * piece + side * half_piece
        return final.at[side_core, pl.ds(pl.multiple_of(first, half_piece), half_piece)]

    def final_rows(side_core, quarter):
        return final.at[side_core, rows_of(quarter, piece)]

    place = final_rows(core, dp)
    start(place, place, "fx", "dp", x_peer)
    start(place, place, "fy", "dp", y_peer)
    start(place, place, "fs0", "seq", sibling)
    place = final_rows(core, x_peer)
    arrived(place, "fx")
    part = final_half(core, x_peer, 0)
    start(part, part, "ffy", "dp", y_peer)
    start(place, place, "fsx", "seq", sibling)
    place = final_rows(core, y_peer)
    arrived(place, "fy")
    part = final_half(core, y_peer, 1)
    start(part, part, "ffx", "dp", x_peer)
    start(place, place, "fsy", "seq", sibling)
    for side, name in ((0, "y"), (1, "x")):
        part = final_half(core, diagonal, side)
        arrived(part, "ff" + name)
        start(part, part, "ffs" + name, "seq", sibling)
    arrived(final_rows(sibling, dp), "fs0")
    arrived(final_rows(sibling, x_peer), "fsx")
    arrived(final_rows(sibling, y_peer), "fsy")
    arrived(final_half(sibling, diagonal, 0), "ffsy")
    arrived(final_half(sibling, diagonal, 1), "ffsx")

    factor = token_count ** (-0.5)
    for at, ref in enumerate((gq_ref, gk_ref, gv_ref, go_ref)):
        for side in (0, 1):
            ref[:, side * half : (side + 1) * half] = (
                final[side, :, at * half : (at + 1) * half].astype(F32) * factor
            )
    for one in sends:
        one.wait_send()


def fused_body(signal, w_query, w_key, w_value, w_output, upstream):
    frames, width = signal.shape[1:]
    block, heads_width = w_query.shape
    both, half = 2 * frames, heads_width // 2
    n_dp, n_z = lax.axis_size("dp"), lax.axis_size("fsdp")
    piece = block // n_dp
    token_count = signal.shape[0] * n_dp * n_z * both
    vmem = pl.BlockSpec(memory_space=pltpu.VMEM)
    rows_shape = jax.ShapeDtypeStruct((frames, width), BF16)
    grad_shape = jax.ShapeDtypeStruct((block, heads_width), F32)

    def kernel(*refs):
        fused_kernel(token_count, *refs)

    output_rows, grad_rows, *grads = pl.pallas_call(
        kernel,
        out_shape=[rows_shape, rows_shape] + [grad_shape] * 4,
        in_specs=[vmem] * 2,
        out_specs=[vmem] * 6,
        scratch_shapes=[
            pltpu.VMEM((width, 4 * half), BF16),
            pltpu.VMEM((both, width), BF16),
            pltpu.VMEM((both, width), BF16),
            pltpu.VMEM((both, width), BF16),
            pltpu.VMEM((both, 3 * half), F32),
            pltpu.VMEM((both, half), F32),
            pltpu.VMEM((both, half), BF16),
            pltpu.VMEM((both, 3 * half), BF16),
            pltpu.VMEM((n_z, block, 4 * half), BF16),
            pltpu.VMEM((n_z, 2, piece // 2, 4 * half), BF16),
            pltpu.VMEM((n_z, 2, piece // 2, 4 * half), BF16),
            pltpu.VMEM((n_z, 2, 2, piece // 2, 4 * half), BF16),
            pltpu.VMEM((n_z, piece, 4 * half), BF16),
            pltpu.VMEM((n_z - 1, piece, 4 * half), BF16),
            pltpu.VMEM((2, block, 4 * half), BF16),
            pltpu.VMEM((frames, width), F32),
            pltpu.VMEM((frames, width), F32),
            pltpu.VMEM((frames, width), F32),
            pltpu.VMEM((frames, width), F32),
            pltpu.SemaphoreType.DMA((N_SEMS,)),
            pltpu.SemaphoreType.DMA((N_SEMS,)),
        ],
        compiler_params=pltpu.CompilerParams(
            collective_id=0, has_side_effects=True, vmem_limit_bytes=44 * 1024 * 1024
        ),
    )(
        jnp.concatenate([signal[0], upstream[0]], axis=0),
        jnp.concatenate([w_query, w_key, w_value, w_output], axis=0),
    )
    return (output_rows[None], grad_rows[None], *grads)


def fits(mesh):
    return mesh.shape["dp"] == 4 and mesh.shape["seq"] == 2 and mesh.shape["fsdp"] == 4


def solution(mesh):
    placed = (
        P(("dp", "fsdp"), "seq", None),
        P("fsdp", None),
        P("fsdp", None),
        P("fsdp", None),
        P("fsdp", None),
        P(("dp", "fsdp"), "seq", None),
    )
    return jax.shard_map(
        fused_body if fits(mesh) else body,
        mesh=mesh,
        in_specs=placed,
        out_specs=(
            P(("dp", "fsdp"), "seq", None),
            P(("dp", "fsdp"), "seq", None),
            P("fsdp", None),
            P("fsdp", None),
            P("fsdp", None),
            P("fsdp", None),
        ),
        check_vma=False,
    )
```
